256 devices in a mesh: slab: 64 (over y, z, core), tile: 4 (over x).
Axes of the slice: x: 4, y: 4, z: 8, core: 2. Of those that a mesh axis runs over, the one named last changes fastest.
Arguments:
- positions: bfloat16 [16384, 3, 128], P('slab'), may hold values from 0 to 2
- charges: bfloat16 [16384, 128], P('slab'), may hold values from -0.1796875 to 0.1796875
- leaf_counts: int32 [16384], P('slab'), may hold values from 16 to 128
- multipoles: bfloat16 [16384, 128], P('slab'), may hold values from -6 to 6
- m2l_ops: bfloat16 [316, 128, 128], P('tile'), may hold values from -0.0390625 to 0.0390625
- leaf_send: int32 [576, 256], P('slab', 'tile'), may hold values from -1 to 255, as said below
- pair_slots: int32 [16384, 28], P('slab', 'tile'), may hold values from -1 to 575, as said below
- far_send: int32 [576, 768], P('slab', 'tile'), may hold values from -1 to 255, as said below
- far_slots: int32 [16384, 316], P('slab', 'tile'), may hold values from -1 to 1727, as said below
Outputs:
- near_potential: float32 [16384, 128], P(('slab', 'tile'))
- local_expansion: float32 [16384, 128], P(('slab', 'tile'))
The draws below stay inside these ranges and needn't reach their ends.
Inputs may be any that keep to these rules, and one draw needn't show every extreme that they name: `leaf_send`: row s * 9 + k, columns t * 64 to t * 64 + 63, lists the local leaves that tile t of slab s sends to tile t of slab s + k - 4: when that slab exists, one to 64 live slots first, then -1; rows for slabs outside the mesh are all -1; every receiving device gets 64 leaves from at least one slab. `pair_slots`: columns t * 7 onward belong to tile t and name a received slot k * 64 + c that is live in leaf_send for sending slab r - k + 4, or -1 for an empty column; every live received slot is named by some column. `far_send`: as leaf_send, for multipoles with 192 slots a route and tile. `far_slots`: columns t * 79 onward belong to tile t and name a received multipole slot k * 192 + c that is live in far_send, or -1; every live received slot is named.
All inputs are finite; a program needn't handle non-finite values.
Results may differ from the reference program's by a relative error of at most 0.00035.
Values may be sent and summed in bfloat16 or wider, within the bound.
No kernel may reach another device: no remote copies, remote signals or barrier semaphores. Data moves between devices by JAX's collectives and lax.ppermute only.
A program may use at most 64 MiB of HBM per device.

```python
import jax
import jax.numpy as jnp
from jax import lax

LEAF_SIZE = 128
MULT = 128
NB = 28
OPS = 316
LEAF_SLAB = 256
REACH = 4
CAP = 64
CAPM = 192
LEAVES = 16384
N_SLAB = 64
N_TILE = 4


def route_plan(key, capacity, columns):
    peer_count = 2 * REACH + 1
    subkeys = jax.random.split(key, 7)
    offsets = jnp.arange(peer_count, dtype=jnp.int32)
    slabs = jnp.arange(N_SLAB, dtype=jnp.int32)
    receiver_of = slabs[:, None] + offsets[None, :] - REACH
    send_ok = (receiver_of >= 0) & (receiver_of < N_SLAB)
    counts = jax.random.randint(subkeys[0], (N_TILE, N_SLAB, peer_count), 1, capacity + 1)
    forced_k = jax.random.randint(subkeys[1], (N_TILE, N_SLAB), 0, peer_count)
    forced_s = jnp.clip(slabs[None, :] - forced_k + REACH, 0, N_SLAB - 1)
    forced_k = slabs[None, :] - forced_s + REACH
    receiver_safe = jnp.clip(receiver_of, 0, N_SLAB - 1)
    is_forced = send_ok[None, :, :] & (forced_k[:, receiver_safe] == offsets[None, None, :])
    counts = jnp.where(is_forced, capacity, counts)
    counts = jnp.where(send_ok[None, :, :], counts, 0)
    picked = jax.random.randint(subkeys[2], (N_TILE, N_SLAB, peer_count, capacity), 0, LEAF_SLAB)
    slot_ids = jnp.arange(capacity, dtype=jnp.int32)
    filled = slot_ids[None, None, None, :] < counts[..., None]
    send_table = jnp.where(filled, picked, -1)
    send_rows = jnp.transpose(send_table, (1, 2, 0, 3)).reshape(N_SLAB * peer_count, N_TILE * capacity)
    sender_of = slabs[:, None] - offsets[None, :] + REACH
    recv_ok = (sender_of >= 0) & (sender_of < N_SLAB)
    sender_safe = jnp.clip(sender_of, 0, N_SLAB - 1)
    received = filled[:, sender_safe, offsets[None, :], :] & recv_ok[None, :, :, None]
    received = received.reshape(N_TILE, N_SLAB, peer_count * capacity)
    valid_first = jnp.argsort(jnp.where(received, 0, 1), axis=-1, stable=True).astype(jnp.int32)
    valid_count = jnp.sum(received.astype(jnp.int32), axis=-1)
    entries = LEAF_SLAB * columns
    entry_ids = jnp.arange(entries, dtype=jnp.int32)
    spare_pick = jax.random.randint(subkeys[3], (N_TILE, N_SLAB, entries), 0, 1 << 20) % valid_count[..., None]
    is_base = entry_ids[None, None, :] < valid_count[..., None]
    chosen = jnp.where(is_base, entry_ids[None, None, :], spare_pick)
    slot_table = jnp.take_along_axis(valid_first, chosen, axis=-1)
    threshold = jax.random.randint(subkeys[4], (N_TILE, N_SLAB, 1), 4, 21)
    is_kept = is_base | (jax.random.randint(subkeys[5], (N_TILE, N_SLAB, entries), 0, 20) < threshold)
    slot_table = jnp.where(is_kept, slot_table, -1)
    scores = jax.random.randint(subkeys[6], (N_TILE, N_SLAB, entries), 0, 1 << 12) * entries + entry_ids[None, None, :]
    shuffle = jnp.argsort(scores, axis=-1).astype(jnp.int32)
    slot_table = jnp.take_along_axis(slot_table, shuffle, axis=-1)
    slot_rows = jnp.transpose(slot_table.reshape(N_TILE, N_SLAB, LEAF_SLAB, columns), (1, 2, 0, 3)).reshape(LEAF_SLAB * N_SLAB, N_TILE * columns)
    return (send_rows.astype(jnp.int32), slot_rows.astype(jnp.int32))


def draw_leaf_send(key, part):
    return route_plan(jax.random.fold_in(key, 11), CAP, NB // N_TILE)[0]


def draw_pair_slots(key, part):
    return route_plan(jax.random.fold_in(key, 11), CAP, NB // N_TILE)[1]


def draw_far_send(key, part):
    return route_plan(jax.random.fold_in(key, 23), CAPM, OPS // N_TILE)[0]


def draw_far_slots(key, part):
    return route_plan(jax.random.fold_in(key, 23), CAPM, OPS // N_TILE)[1]


def plant(values, own_key, low, top_value):
    longest = values.shape.index(max(values.shape))
    spots = []
    for shift in (0, 1):
        where = [jax.random.randint(jax.random.fold_in(own_key, axis), (), 0, length) for axis, length in enumerate(values.shape)]
        where[longest] = (where[longest] + shift) % values.shape[longest]
        spots.append(tuple(where))
    return values.at[spots[0]].set(low).at[spots[1]].set(top_value)


def steps_of(rng, shape, cuts, low, largest):
    level = 1.0
    for dim, blocks in cuts:
        draws = jax.random.uniform(jax.random.fold_in(jax.random.fold_in(rng, 6), dim), (blocks,), jnp.float32, low / len(cuts), largest / len(cuts))
        level = level * jnp.repeat(jnp.exp(draws), shape[dim] // blocks).reshape((-1,) + (1,) * (len(shape) - 1 - dim))
    return level


def scatter_about(own_key, dims, deviation, bound, shards=(), kind=jnp.bfloat16):
    gain = steps_of(own_key, dims, shards, -0.22, 0.18) if shards else 1.0
    values = jax.random.normal(own_key, dims, jnp.float32) * deviation * gain
    return jnp.minimum(jnp.maximum(values, -bound), bound).astype(kind)


def setup_inputs(seed: int = 0) -> dict:
    splits = jax.random.split(jax.random.key(seed), 10)
    return {
        "positions": jnp.clip(2.0 * jax.random.uniform(splits[0], (LEAVES, 3, LEAF_SIZE), jnp.float32) ** steps_of(splits[0], (LEAVES, 3, LEAF_SIZE), ((0, 64),), -0.2, 0.2), 0.0, 2.0).astype(jnp.bfloat16),
        "charges": scatter_about(splits[1], (LEAVES, LEAF_SIZE), 0.03, 0.1796875, ((0, 64),)),
        "leaf_counts": plant(jax.random.randint(splits[2], (LEAVES,), LEAF_SIZE // 8, LEAF_SIZE + 1), jax.random.fold_in(splits[2], 1), LEAF_SIZE // 8, LEAF_SIZE).astype(jnp.int32),
        "multipoles": scatter_about(splits[3], (LEAVES, MULT), 1.0, 6.0, ((0, 64),)),
        "m2l_ops": scatter_about(splits[4], (OPS, MULT, MULT), (MULT * 189) ** -0.5, 0.0390625, ((0, 4),)),
        "leaf_send": draw_leaf_send(jax.random.fold_in(splits[9], 71), 0),
        "pair_slots": draw_pair_slots(jax.random.fold_in(splits[9], 71), 0),
        "far_send": draw_far_send(jax.random.fold_in(splits[9], 71), 0),
        "far_slots": draw_far_slots(jax.random.fold_in(splits[9], 71), 0),
    }


def pair_block(operands):
    target_pos, source_pos, source_q = operands
    distance = jnp.zeros((source_pos.shape[0], source_pos.shape[1], target_pos.shape[2], source_pos.shape[3]), jnp.float32)
    for coord in range(3):
        delta = target_pos[:, None, coord, :, None] - source_pos[:, :, coord, None, :]
        distance = distance + delta * delta
    inverse = lax.rsqrt(distance + 0.09)
    return lax.optimization_barrier(jnp.sum(inverse * source_q[:, :, None, :], axis=(1, 3)))

def near_field(targets, sources, source_q):
    leaf_total = targets.shape[0]
    block_leaves = min(16, leaf_total)
    block_count = leaf_total // block_leaves
    result = lax.map(pair_block, (targets.reshape((block_count, block_leaves) + targets.shape[1:]), sources.reshape((block_count, block_leaves) + sources.shape[1:]), source_q.reshape((block_count, block_leaves) + source_q.shape[1:])))
    return result.reshape(leaf_total, targets.shape[2])

def resolve(slot_rows, send_table, capacity, columns, slab):
    peer_count = 2 * REACH + 1
    column_tile = (jnp.arange(slot_rows.shape[1], dtype=jnp.int32) // columns)[None, :]
    flat_slot = jnp.maximum(slot_rows, 0)
    offset = flat_slot // capacity
    within = flat_slot % capacity
    sender = jnp.clip(slab - offset + REACH, 0, N_SLAB - 1).astype(jnp.int32)
    local_leaf = jnp.maximum(send_table[sender * peer_count + offset, column_tile * capacity + within], 0)
    return ((sender * LEAF_SLAB + local_leaf).astype(jnp.int32), slot_rows >= 0)

def reference(positions, charges, leaf_counts, multipoles, m2l_ops, leaf_send, pair_slots, far_send, far_slots):
    lane_ids = jnp.arange(LEAF_SIZE, dtype=jnp.int32)
    charge_mask = lane_ids[None, :] < leaf_counts[:, None]
    source_q = jnp.where(charge_mask, charges.astype(jnp.float32), jnp.zeros((), jnp.float32))
    coords = positions.astype(jnp.float32)
    operators = m2l_ops.reshape(OPS * MULT, MULT)

    def slab_work(slab):
        start = (slab * LEAF_SLAB).astype(jnp.int32)
        pair_rows = lax.dynamic_slice_in_dim(pair_slots, start, LEAF_SLAB, 0)
        near_src, near_live = resolve(pair_rows, leaf_send, CAP, NB // N_TILE, slab)
        source_pos = coords[near_src]
        live_q = jnp.where(near_live[:, :, None], source_q[near_src], jnp.zeros((), jnp.float32))
        targets = lax.dynamic_slice_in_dim(coords, start, LEAF_SLAB, 0)
        near = near_field(targets, source_pos, live_q)
        target_mask = lax.dynamic_slice_in_dim(charge_mask, start, LEAF_SLAB, 0)
        near = jnp.where(target_mask, near, jnp.zeros((), jnp.float32))
        far_rows = lax.dynamic_slice_in_dim(far_slots, start, LEAF_SLAB, 0)
        far_src, far_live = resolve(far_rows, far_send, CAPM, OPS // N_TILE, slab)
        regrouped = jnp.where(far_live[:, :, None], multipoles[far_src], jnp.zeros((), jnp.bfloat16))
        local = jnp.dot(regrouped.reshape(LEAF_SLAB, OPS * MULT), operators, preferred_element_type=jnp.float32)
        return (near, local)
    near_all, local_all = lax.map(slab_work, jnp.arange(N_SLAB, dtype=jnp.int32))
    return (near_all.reshape(LEAVES, LEAF_SIZE), local_all.reshape(LEAVES, MULT))
```

```python
import numpy as np
import jax
import jax.numpy as jnp
from jax import lax
from jax.experimental import pallas as pl
from jax.experimental.pallas import tpu as pltpu
from jax.sharding import PartitionSpec as P

F32 = jnp.float32
BF16 = jnp.bfloat16
VM = pl.BlockSpec(memory_space=pltpu.VMEM)
SM = pl.BlockSpec(memory_space=pltpu.SMEM)

def dot(a, b, dims=((1,), (0,))):
    return lax.dot_general(a, b, (dims, ((), ())), preferred_element_type=F32)


def pack_kernel(pos_ref, charge_ref, count_ref, multi_ref, leaf_ref, far_ref, *out_refs):
    peers, cap = leaf_ref.shape
    capm = far_ref.shape[1]
    leaves, lanes = charge_ref.shape
    lane = lax.broadcasted_iota(jnp.int32, (leaves, lanes), 1)
    live = lane < count_ref[...]
    masked = jnp.where(live, charge_ref[...].astype(F32), 0.0).astype(BF16)
    table = jnp.concatenate([pos_ref[0], pos_ref[1], pos_ref[2], masked], axis=1)
    box = lax.broadcasted_iota(jnp.int32, (leaves, cap), 0)
    boxm = lax.broadcasted_iota(jnp.int32, (leaves, capm), 0)
    multi = multi_ref[...]
    for k in range(peers):
        pick = jnp.where(box == leaf_ref[k:k + 1, :], 1.0, 0.0).astype(BF16)
        rows = dot(pick, table, ((0,), (0,))).astype(BF16)
        for c in range(4):
            out_refs[k][c * cap:(c + 1) * cap, :] = rows[:, c * lanes:(c + 1) * lanes]
        pickm = jnp.where(boxm == far_ref[k:k + 1, :], 1.0, 0.0).astype(BF16)
        out_refs[k][4 * cap:4 * cap + capm, :] = dot(pickm, multi, ((0,), (0,))).astype(BF16)


def near_kernel(slot_ref, count_ref, pos_ref, perm_s_ref, perm_t_ref, *refs):
    got = refs[:9]
    out_ref, w_ref, q_ref, lhs_ref = refs[9:]
    leaves, lanes = out_ref.shape
    columns = slot_ref.shape[0]
    cap = 64
    slots = 9 * cap
    one = jnp.ones((16, lanes), BF16)
    zero = jnp.zeros((16, lanes), BF16)

    def split(x, y, z, bias):
        x, y, z = x.astype(F32), y.astype(F32), z.astype(F32)
        total = x * x + y * y + z * z + bias
        hi = total.astype(BF16)
        rest = total - hi.astype(F32)
        mid = rest.astype(BF16)
        return hi, mid, (rest - mid.astype(F32)).astype(BF16)

    for k in range(9):
        for g in range(cap // 16):
            x, y, z, q = [got[k][c * cap + g * 16:c * cap + g * 16 + 16, :] for c in range(4)]
            hi, mid, lo = split(x, y, z, 0.09)
            stack = jnp.concatenate([x, y, z, hi, mid, lo, one, zero], axis=0)
            tiles = dot(perm_s_ref[...], stack).astype(BF16)
            w_ref[k * cap + g * 16:k * cap + g * 16 + 16] = tiles.reshape(16, 16, lanes)
            q_ref[k * cap + g * 16:k * cap + g * 16 + 16, :] = q.astype(F32)
    w_ref[slots] = one
    q_ref[slots:slots + 8, :] = jnp.zeros((8, lanes), F32)

    for g in range(leaves // 16):
        x, y, z = [pos_ref[c, g * 16:g * 16 + 16, :] for c in range(3)]
        hi, mid, lo = split(x, y, z, 0.0)
        stack = jnp.concatenate([x, y, z, hi, mid, lo, one, zero], axis=0)
        feat = dot(stack, perm_t_ref[...], ((0,), (0,)))
        for j in range(8):
            lhs_ref[g * 8 + j] = feat[:, j * 32:j * 32 + 32].astype(BF16)

    lane_row = lax.broadcasted_iota(jnp.int32, (1, lanes), 1)

    def pair(p, _):
        l0 = 2 * p
        tiles = []
        charge = []
        for a in range(2):
            for n in range(columns):
                s = slot_ref[n, l0 + a]
                s = jnp.where(s < 0, slots, s)
                t = w_ref[s]
                tiles.append(jnp.concatenate([t, zero] if a == 0 else [zero, t], axis=0))
                charge.append(q_ref[pl.ds(s, 1), :])
        r2 = dot(lhs_ref[p], jnp.concatenate(tiles, axis=1))
        inv = lax.rsqrt(r2)
        for a in range(2):
            acc = jnp.zeros((lanes, lanes), F32)
            for n in range(columns):
                i = a * columns + n
                acc = acc + inv[:, i * lanes:(i + 1) * lanes] * charge[i]
            row = jnp.sum(acc.T, axis=0, keepdims=True)
            row = jnp.where(lane_row < count_ref[l0 + a], row, 0.0)
            out_ref[pl.ds(l0 + a, 1), :] = row
        return 0

    lax.fori_loop(0, leaves // 2, pair, 0, unroll=2)


def perms():
    s = np.zeros((256, 128), np.float32)
    t = np.zeros((128, 256), np.float32)
    plane_s = [(0, -2.0), (1, -2.0), (2, -2.0), (3, 1.0), (4, 1.0), (5, 1.0), (6, 1.0), (6, 1.0), (6, 1.0)]
    plane_t = [(0, 1.0), (1, 1.0), (2, 1.0), (6, 1.0), (6, 1.0), (6, 1.0), (3, 1.0), (4, 1.0), (5, 1.0)]
    for j in range(16):
        for p, (plane, v) in enumerate(plane_s):
            s[16 * j + p, plane * 16 + j] = v
        for p, (plane, v) in enumerate(plane_t):
            t[plane * 16 + j, 16 * j + p] = v
    return jnp.asarray(s, BF16), jnp.asarray(t, BF16)


def far_kernel(tile_ref, slot_ref, m2l_ref, near_ref, *refs):
    got = refs[:9]
    part_refs = refs[9:13]
    out_ref, table_ref, hot_ref = refs[13:]
    ops, leaves = slot_ref.shape
    capm = 192
    lanes = out_ref.shape[1]
    half = table_ref.shape[0]
    table_ref[...] = jnp.zeros_like(table_ref)
    for k in range(9):
        for h in range(2):
            lo, hi = max(k * capm, h * half), min((k + 1) * capm, (h + 1) * half)
            if lo < hi:
                table_ref[lo - h * half:hi - h * half, h * lanes:(h + 1) * lanes] = \
                    got[k][256 + lo - k * capm:256 + hi - k * capm, :]
    out_ref[...] = jnp.zeros_like(out_ref)
    lane0 = lax.broadcasted_iota(jnp.int32, (leaves, lanes), 1)
    iota0 = lane0.astype(F32).astype(BF16)
    iota1 = (lane0 + lanes).astype(F32).astype(BF16)
    one = jnp.ones((leaves, lanes), BF16)
    zero = jnp.zeros((leaves, lanes), BF16)

    def chunk(start, n):
        st = slot_ref[pl.ds(start, n), :].astype(F32)
        if n < 8:
            st = jnp.concatenate([st, jnp.full((8 - n, leaves), -1.0, F32)], axis=0)
        st = st.T
        halves = []
        for i in range(n):
            col = jnp.broadcast_to(st[:, i:i + 1], (leaves, lanes))
            upper = col >= half
            halves.append(upper)
            kk = jnp.where(upper, col - half, col)
            for j in range(half // 256):
                v = (kk - 256.0 * j).astype(BF16)
                hot_ref[i * leaves:(i + 1) * leaves, j * 256:j * 256 + 128] = jnp.where(v == iota0, one, zero)
                hot_ref[i * leaves:(i + 1) * leaves, j * 256 + 128:j * 256 + 256] = jnp.where(v == iota1, one, zero)
        both = dot(hot_ref[:n * leaves, :], table_ref[...])
        rows = []
        for i in range(n):
            b = both[i * leaves:(i + 1) * leaves]
            rows.append(jnp.where(halves[i], b[:, lanes:], b[:, :lanes]).astype(BF16))
        mats = m2l_ref[pl.ds(start, n)].reshape(n * lanes, lanes)
        out_ref[...] += dot(jnp.concatenate(rows, axis=1), mats)

    full = ops // 8

    def body(c, _):
        chunk(pl.multiple_of(c * 8, 8), 8)
        return 0

    lax.fori_loop(0, full, body, 0)
    if ops % 8:
        chunk(full * 8, ops % 8)
    rows = leaves // 4
    for d in range(4):
        at = pl.multiple_of(lax.rem(tile_ref[0] + d, 4) * rows, rows)
        part_refs[d][:, :lanes] = near_ref[pl.ds(at, rows), :]
        part_refs[d][:, lanes:] = out_ref[pl.ds(at, rows), :]


def params(mb=24):
    return pltpu.CompilerParams(vmem_limit_bytes=mb * 1024 * 1024)


def pack(pos, charges, counts, multi, leaf_send, far_send):
    peers, cap = leaf_send.shape
    capm = far_send.shape[1]
    return pl.pallas_call(
        pack_kernel, out_shape=[jax.ShapeDtypeStruct((4 * cap + capm, 128), BF16)] * peers,
        in_specs=[VM] * 6, out_specs=[VM] * peers, compiler_params=params(),
    )(pos, charges, counts[:, None], multi, leaf_send, far_send)


def near(slots_t, counts, pos, got):
    s, t = perms()
    return pl.pallas_call(
        near_kernel, out_shape=jax.ShapeDtypeStruct((256, 128), F32),
        in_specs=[SM, SM] + [VM] * (3 + len(got)), out_specs=VM,
        scratch_shapes=[pltpu.VMEM((577, 16, 128), BF16), pltpu.VMEM((584, 128), F32), pltpu.VMEM((128, 128, 32), BF16)],
        compiler_params=params(),
    )(slots_t, counts, pos, s, t, *got)


def far(tile, slots_t, m2l, near_part, got):
    return pl.pallas_call(
        far_kernel, out_shape=[jax.ShapeDtypeStruct((64, 256), F32)] * 4,
        in_specs=[SM] + [VM] * (3 + len(got)), out_specs=[VM] * 4,
        scratch_shapes=[pltpu.VMEM((256, 128), F32), pltpu.VMEM((1024, 256), BF16), pltpu.VMEM((2048, 1024), BF16)],
        compiler_params=params(),
    )(tile, slots_t, m2l, near_part, *got)


def per_device(positions, charges, leaf_counts, multipoles, m2l_ops, leaf_send, pair_slots, far_send, far_slots):
    peers = leaf_send.shape[0]
    reach = (peers - 1) // 2
    slabs = lax.axis_size("slab")
    tiles = lax.axis_size("tile")
    planes = jnp.transpose(positions, (1, 0, 2))
    payload = pack(planes, charges, leaf_counts, multipoles, leaf_send, far_send)
    got = list(payload)
    for step in range(reach, 0, -1):
        for k in (reach + step, reach - step):
            hops = k - reach
            got[k] = lax.ppermute(payload[k], "slab", [(s, (s + hops) % slabs) for s in range(slabs)])
    near_part = near(pair_slots.T, leaf_counts, planes, got)
    tile = lax.axis_index("tile").astype(jnp.int32).reshape(1)
    parts = far(tile, far_slots.T, m2l_ops, near_part, got)
    total = parts[0]
    for step in range(1, tiles):
        total = total + lax.ppermute(parts[step], "tile", [(t, (t + step) % tiles) for t in range(tiles)])
    return total[:, :128], total[:, 128:]


def solution(mesh):
    return jax.shard_map(
        per_device,
        mesh=mesh,
        in_specs=(
            P("slab", None, None),
            P("slab", None),
            P("slab"),
            P("slab", None),
            P("tile", None, None),
            P("slab", "tile"),
            P("slab", "tile"),
            P("slab", "tile"),
            P("slab", "tile"),
        ),
        out_specs=(P(("slab", "tile"), None), P(("slab", "tile"), None)),
        check_vma=False,
    )
```

```python
import jax
import jax.numpy as jnp
from jax import lax
from jax.experimental import pallas as pl
from jax.experimental.pallas import tpu as pltpu
from jax.sharding import PartitionSpec as P

F32 = jnp.float32
BF16 = jnp.bfloat16
I32 = jnp.int32
PEERS, CAP, CAPM = 9, 64, 192
LEAVES, LANES = 256, 128
COLUMNS, OPS = 7, 79
SLOTS = PEERS * CAP
CHUNK = 16
CHUNKS = 5
TABLE = 1024
HBM = pl.BlockSpec(memory_space=pltpu.HBM)
VM = pl.BlockSpec(memory_space=pltpu.VMEM)
SM = pl.BlockSpec(memory_space=pltpu.SMEM)


def dot(a, b, dims=((1,), (0,))):
    return lax.dot_general(a, b, (dims, ((), ())), preferred_element_type=F32)


def iota(shape, dim):
    return lax.broadcasted_iota(I32, shape, dim)


def fetch(pairs, sems):
    copies = [pltpu.make_async_copy(a, b, sems.at[i]) for i, (a, b) in enumerate(pairs)]
    for c in copies:
        c.start()
    return copies


def params(mb):
    return pltpu.CompilerParams(vmem_limit_bytes=mb * 1024 * 1024)


def column(row):
    return jnp.broadcast_to(row.astype(F32), (8, LEAVES)).T[:, 0:1]


def pack_kernel(pos_h, charge_h, count_h, multi_h, leaf_h, far_h, *refs):
    out_refs = refs[:PEERS]
    pos, charge, count, multi_ref, leaf, far_s, sems = refs[PEERS:]
    for c in fetch([(pos_h, pos), (charge_h, charge), (count_h, count), (multi_h, multi_ref), (leaf_h, leaf), (far_h, far_s)], sems):
        c.wait()
    live = iota((LEAVES, LANES), 1).astype(F32) < column(count[...])
    masked = jnp.where(live, charge[...].astype(F32), 0.0).astype(BF16)
    table = jnp.concatenate([pos[0], pos[1], pos[2], masked], axis=1)
    box = iota((LEAVES, CAP), 0)
    boxm = iota((LEAVES, CAPM), 0)
    multi = multi_ref[...]
    for k in range(PEERS):
        pick = jnp.where(box == leaf[k:k + 1, :], 1.0, 0.0).astype(BF16)
        rows = dot(pick, table, ((0,), (0,))).astype(BF16)
        for c in range(4):
            out_refs[k][c * CAP:(c + 1) * CAP, :] = rows[:, c * LANES:(c + 1) * LANES]
        pickm = jnp.where(boxm == far_s[k:k + 1, :], 1.0, 0.0).astype(BF16)
        out_refs[k][4 * CAP:4 * CAP + CAPM, :] = dot(pickm, multi, ((0,), (0,))).astype(BF16)


def pack(planes, charges, count_row, multi, leaf_send, far_send):
    return pl.pallas_call(
        pack_kernel,
        out_shape=[jax.ShapeDtypeStruct((4 * CAP + CAPM, LANES), BF16)] * PEERS,
        in_specs=[HBM] * 6,
        out_specs=[VM] * PEERS,
        scratch_shapes=[
            pltpu.VMEM((3, LEAVES, LANES), BF16), pltpu.VMEM((LEAVES, LANES), BF16), pltpu.VMEM((1, LEAVES), I32),
            pltpu.VMEM((LEAVES, LANES), BF16), pltpu.VMEM((PEERS, CAP), I32), pltpu.VMEM((PEERS, CAPM), I32),
            pltpu.SemaphoreType.DMA((6,)),
        ],
        compiler_params=params(56),
        name="pack",
    )(planes, charges, count_row, multi, leaf_send, far_send)


def squares(x, y, z, bias):
    x, y, z = x.astype(F32), y.astype(F32), z.astype(F32)
    total = x * x + y * y + z * z + bias
    hi = total.astype(BF16)
    rest = total - hi.astype(F32)
    mid = rest.astype(BF16)
    return hi, mid, (rest - mid.astype(F32)).astype(BF16)


def spread(transposed, scale, order):
    shape = (128, 256) if transposed else (256, 128)
    big, small = iota(shape, 1 if transposed else 0), iota(shape, 0 if transposed else 1)
    feature, item = big & 15, big >> 4
    plane, item2 = small >> 4, small & 15
    value = jnp.zeros(shape, F32)
    for f, (p, v) in enumerate(order):
        value = jnp.where((feature == f) & (plane == p), v * scale if p < 3 else v, value)
    return jnp.where(item == item2, value, 0.0).astype(BF16)


def prep_kernel(pos_h, count_h, slot_h, pair_h, own_h, lhs_ref, order_ref, code_ref, base_ref, pair_ref, own_ref, pos, count, slot, pair, sems):
    copies = fetch([(pos_h, pos), (count_h, count), (slot_h, slot), (pair_h, pair), (own_h, own_ref)], sems)
    for c in copies:
        c.wait()
    leaf_row = iota((1, LEAVES), 1).astype(F32)
    key_row = count[...].astype(F32) * LEAVES + leaf_row
    key_col = jnp.broadcast_to(key_row, (8, LEAVES)).T[:, 0:1]
    rank = jnp.sum(jnp.where(key_col > key_row, 1.0, 0.0), axis=0, keepdims=True)
    move = jnp.where(rank == iota((LEAVES, LEAVES), 0).astype(F32), 1.0, 0.0).astype(BF16)
    order_ref[...] = dot(jnp.broadcast_to(leaf_row, (8, LEAVES)).astype(BF16), move, ((1,), (1,))).astype(I32)
    pair_ref[:COLUMNS, :] = jnp.where(pair[...] < 0, SLOTS, pair[...])
    pair_ref[COLUMNS:, :] = count[...]
    x, y, z = [dot(move, pos[c]).astype(BF16) for c in range(3)]
    hi, mid, lo = squares(x, y, z, 0.0)
    one = jnp.ones((16, LANES), BF16)
    zero = jnp.zeros((16, LANES), BF16)
    layout = spread(True, 1.0, [(0, 1.0), (1, 1.0), (2, 1.0), (6, 1.0), (6, 1.0), (6, 1.0), (3, 1.0), (4, 1.0), (5, 1.0)])
    for g in range(LEAVES // 16):
        at = slice(g * 16, g * 16 + 16)
        stack = jnp.concatenate([x[at], y[at], z[at], hi[at], mid[at], lo[at], one, zero], axis=0)
        feat = dot(stack, layout, ((0,), (0,)))
        for j in range(8):
            lhs_ref[g * 8 + j] = feat[:, j * 32:j * 32 + 32].astype(BF16)
    s = slot[...]
    base = jnp.int32(0)
    place = s
    for k in range(PEERS):
        here = (s >= k * CAPM) & (s < (k + 1) * CAPM)
        count_k = jnp.max(jnp.where(here, s - (k * CAPM - 1), 0))
        base_ref[k] = base
        place = jnp.where(here, s + (base - k * CAPM), place)
        base = base + ((count_k + 15) & -16)
    base_ref[PEERS] = base
    row = ((place >> 9) << 8) + (place & 255)
    power = jnp.where(row >= 512, 16.0, 1.0) * jnp.where((row & 256) > 0, 4.0, 1.0) * jnp.where((row & 128) > 0, 2.0, 1.0)
    code = (1.0 + (row & 127).astype(F32) * (1.0 / 128.0)) * power
    code = jnp.where((place & 256) > 0, -code, code)
    code = jnp.where(s >= 0, code, 0.0)
    dead = jnp.zeros((1, LEAVES), F32)
    last = (CHUNKS - 1) * CHUNK
    code = jnp.concatenate([code[:last], dead, code[last:], jnp.zeros((LANES - CHUNKS * CHUNK, LEAVES), F32)], axis=0)
    code_ref[...] = code.T


def prep(planes, count_row, far_slots, pair_slots, own):
    return pl.pallas_call(
        prep_kernel,
        out_shape=[
            jax.ShapeDtypeStruct((LEAVES // 2, LANES, 32), BF16), jax.ShapeDtypeStruct((8, LEAVES), I32),
            jax.ShapeDtypeStruct((LEAVES, LANES), F32), jax.ShapeDtypeStruct((16,), I32),
            jax.ShapeDtypeStruct((COLUMNS + 1, LEAVES), I32), jax.ShapeDtypeStruct(own.shape, BF16),
        ],
        in_specs=[HBM] * 5,
        out_specs=[VM, VM, VM, SM, VM, VM],
        scratch_shapes=[
            pltpu.VMEM((3, LEAVES, LANES), BF16), pltpu.VMEM((1, LEAVES), I32), pltpu.VMEM((OPS, LEAVES), I32),
            pltpu.VMEM((COLUMNS, LEAVES), I32), pltpu.SemaphoreType.DMA((5,)),
        ],
        compiler_params=params(24),
        name="prep",
    )(planes, count_row, far_slots, pair_slots, own)


def near_kernel(order, slot, lhs_ref, *refs):
    got = refs[:PEERS]
    out_ref, w_ref, q_ref = refs[PEERS:]
    one = jnp.ones((16, LANES), BF16)
    zero = jnp.zeros((16, LANES), BF16)
    layout = spread(False, -2.0, [(0, 1.0), (1, 1.0), (2, 1.0), (3, 1.0), (4, 1.0), (5, 1.0), (6, 1.0), (6, 1.0), (6, 1.0)])
    for k in range(PEERS):
        x, y, z, q = [got[k][c * CAP:(c + 1) * CAP, :] for c in range(4)]
        hi, mid, lo = squares(x, y, z, 0.09)
        q_ref[k * CAP:(k + 1) * CAP, :] = q.astype(F32)
        for g in range(CAP // 16):
            at = slice(g * 16, g * 16 + 16)
            stack = jnp.concatenate([x[at], y[at], z[at], hi[at], mid[at], lo[at], one, zero], axis=0)
            w_ref[k * CAP + g * 16:k * CAP + g * 16 + 16] = dot(layout, stack).astype(BF16).reshape(16, 16, LANES)
    w_ref[SLOTS] = one
    q_ref[SLOTS:SLOTS + 8, :] = jnp.zeros((8, LANES), F32)
    lane_row = iota((1, LANES), 1)
    group = 16

    def pair(p, rows):
        tiles, charge, leaf = [], [], []
        for a in range(2):
            leaf.append(order[0, 2 * p + a])
            for n in range(COLUMNS):
                s = slot[n, leaf[a]]
                t = w_ref[s]
                tiles.append(jnp.concatenate([t, zero] if a == 0 else [zero, t], axis=0))
                charge.append(q_ref[pl.ds(s, 1), :])
        lhs = lhs_ref[p][:rows]
        acc = [None, None]
        for i in range(0, 2 * COLUMNS, 2):
            inv = lax.rsqrt(dot(lhs, jnp.concatenate(tiles[i:i + 2], axis=1)))
            for j in (i, i + 1):
                a = j // COLUMNS
                term = inv[:, (j - i) * LANES:(j - i + 1) * LANES] * charge[j]
                acc[a] = term if acc[a] is None else acc[a] + term
        for a in range(2):
            full = acc[a]
            if rows < LANES:
                full = jnp.concatenate([full, jnp.zeros((LANES - rows, LANES), F32)], axis=0)
            row = jnp.sum(full.T, axis=0, keepdims=True)
            out_ref[pl.ds(leaf[a], 1), :] = jnp.where(lane_row < slot[COLUMNS, leaf[a]], row, 0.0)

    def body(g, _):
        most = slot[COLUMNS, order[0, g * group]]
        for rows in range(STEP, LANES + 1, STEP):
            @pl.when((most > rows - STEP) & (most <= rows))
            def _():
                for p in range(group // 2):
                    pair(g * (group // 2) + p, rows)
        return 0

    lax.fori_loop(0, LEAVES // group, body, 0)


STEP = 32


def near(order, pair, lhs, got):
    return pl.pallas_call(
        near_kernel,
        out_shape=jax.ShapeDtypeStruct((LEAVES, LANES), F32),
        in_specs=[SM] * 2 + [VM] * (1 + PEERS),
        out_specs=VM,
        scratch_shapes=[
            pltpu.VMEM((SLOTS + 1, 16, LANES), BF16), pltpu.VMEM((SLOTS + 8, LANES), F32),
        ],
        compiler_params=params(24),
        name="near",
    )(order, pair, lhs, *got)


def far_kernel(tile_ref, base_ref, code_ref, m2l_h, near_ref, *refs):
    got = refs[:PEERS]
    part_refs = refs[PEERS:PEERS + 4]
    local, table, whole, m2l, sems = refs[PEERS + 4:]
    copies = fetch([(m2l_h, m2l)], sems)
    table[...] = jnp.zeros_like(table)
    for k in range(PEERS):
        for b in range(CAPM // 16):
            at = base_ref[k] + 16 * b
            row = pl.multiple_of(((at >> 9) << 8) + (at & 255), 16)
            table[(at >> 8) & 1, pl.ds(row, 16), :] = got[k][4 * CAP + 16 * b:4 * CAP + 16 * b + 16, :]
    local[...] = jnp.zeros_like(local)
    whole[:, :LANES] = table[0]
    whole[:, LANES:] = table[1]
    lane = iota((1, LANES), 1).astype(F32) * (1.0 / 128.0) + 1.0

    def run(depth):
        marks = [jnp.broadcast_to((lane * (2.0 ** j)).astype(BF16), (LEAVES, LANES)) for j in range(depth // LANES)]

        def body(c, _):
            code = pltpu.roll(code_ref[...], lax.rem(LANES - c * CHUNK, LANES), 1)[:, :CHUNK]
            weights = whole[:depth]
            mats = m2l[pl.ds(jnp.minimum(c * CHUNK, OPS - CHUNK), CHUNK)].reshape(CHUNK * LANES, LANES)
            rows = []
            for i in range(CHUNK):
                col = jnp.broadcast_to(code[:, i:i + 1], (LEAVES, LANES))
                wide = jnp.abs(col.astype(BF16))
                hot = jnp.concatenate([jnp.where(wide == m, jnp.ones_like(wide), jnp.zeros_like(wide)) for m in marks], axis=1)
                both = dot(hot, weights)
                rows.append(jnp.where(col < 0.0, both[:, LANES:], both[:, :LANES]).astype(BF16))
            total = local[...]
            for i in range(0, CHUNK, 8):
                total = total + dot(jnp.concatenate(rows[i:i + 8], axis=1), mats[i * LANES:(i + 8) * LANES])
            local[...] = total
            return 0

        lax.fori_loop(0, CHUNKS, body, 0)

    for c in copies:
        c.wait()
    small = base_ref[PEERS] <= 1536

    @pl.when(small)
    def _():
        run(768)

    @pl.when(jnp.logical_not(small))
    def _():
        run(1024)

    rows = LEAVES // 4
    for d in range(4):
        at = pl.multiple_of(lax.rem(tile_ref[0] + d, 4) * rows, rows)
        part_refs[d][:, :LANES] = near_ref[pl.ds(at, rows), :]
        part_refs[d][:, LANES:] = local[pl.ds(at, rows), :]


def far(tile, base, code, m2l, near_part, got):
    return pl.pallas_call(
        far_kernel,
        out_shape=[jax.ShapeDtypeStruct((LEAVES // 4, 2 * LANES), F32)] * 4,
        in_specs=[SM, SM, VM, HBM, VM] + [VM] * PEERS,
        out_specs=[VM] * 4,
        scratch_shapes=[
            pltpu.VMEM((LEAVES, LANES), F32), pltpu.VMEM((2, TABLE, LANES), BF16),
            pltpu.VMEM((TABLE, 2 * LANES), BF16),
            pltpu.VMEM((OPS, LANES, LANES), BF16), pltpu.SemaphoreType.DMA((1,)),
        ],
        compiler_params=params(32),
        name="far",
    )(tile, base, code, m2l, near_part, *got)


def per_device(positions, charges, leaf_counts, multipoles, m2l_ops, leaf_send, pair_slots, far_send, far_slots):
    reach = (PEERS - 1) // 2
    slabs = lax.axis_size("slab")
    tiles = lax.axis_size("tile")
    planes = jnp.transpose(positions, (1, 0, 2))
    count_row = leaf_counts.reshape(1, LEAVES)
    payload = pack(planes, charges, count_row, multipoles, leaf_send, far_send)
    got = list(payload)
    for step in range(reach, 0, -1):
        for k in (reach + step, reach - step):
            hops = k - reach
            got[k] = lax.ppermute(payload[k], "slab", [(s, (s + hops) % slabs) for s in range(slabs)])
    lhs, order, code, base, pair, got[reach] = prep(planes, count_row, far_slots.T, pair_slots.T, payload[reach])
    near_part = near(order, pair, lhs, got)
    tile = lax.axis_index("tile").astype(I32).reshape(1)
    parts = far(tile, base, code, m2l_ops, near_part, got)
    total = parts[0]
    for step in range(1, tiles):
        total = total + lax.ppermute(parts[step], "tile", [(t, (t + step) % tiles) for t in range(tiles)])
    return total[:, :LANES], total[:, LANES:]


def solution(mesh):
    return jax.shard_map(
        per_device,
        mesh=mesh,
        in_specs=(
            P("slab", None, None),
            P("slab", None),
            P("slab"),
            P("slab", None),
            P("tile", None, None),
            P("slab", "tile"),
            P("slab", "tile"),
            P("slab", "tile"),
            P("slab", "tile"),
        ),
        out_specs=(P(("slab", "tile"), None), P(("slab", "tile"), None)),
        check_vma=False,
    )
```

```python
import jax
import jax.numpy as jnp
from jax import lax
from jax.experimental import pallas as pl
from jax.experimental.pallas import tpu as pltpu
from jax.sharding import PartitionSpec as P

F32 = jnp.float32
BF16 = jnp.bfloat16
I32 = jnp.int32
PEERS, CAP, CAPM = 9, 64, 192
LEAVES, LANES = 256, 128
COLUMNS, OPS = 7, 79
SLOTS = PEERS * CAP
PAYLOAD = 4 * CAP + CAPM
CHUNK = 40
CHUNKS = 2
TABLE = 1024
HBM = pl.BlockSpec(memory_space=pltpu.HBM)
VM = pl.BlockSpec(memory_space=pltpu.VMEM)
SM = pl.BlockSpec(memory_space=pltpu.SMEM)


def dot(a, b, dims=((1,), (0,))):
    return lax.dot_general(a, b, (dims, ((), ())), preferred_element_type=F32)


def iota(shape, dim):
    return lax.broadcasted_iota(I32, shape, dim)


def fetch(pairs, sems):
    copies = [pltpu.make_async_copy(a, b, sems.at[i]) for i, (a, b) in enumerate(pairs)]
    for c in copies:
        c.start()
    return copies


def params(mb):
    return pltpu.CompilerParams(vmem_limit_bytes=mb * 1024 * 1024)


def column(row):
    return jnp.broadcast_to(row.astype(F32), (8, LEAVES)).T[:, 0:1]


def routes():
    reach = (PEERS - 1) // 2
    pairs = [(reach, reach)]
    for step in range(reach, 0, -1):
        pairs += [(reach - step, reach + step), (reach + step, reach - step)]
    return pairs


def arrived(odd, got, k, part):
    reach = (PEERS - 1) // 2
    if k == reach:
        return got[0][part]
    step = abs(k - reach)
    first = 1 + 2 * (reach - step)
    upward = odd == step % 2
    a, b = (first, first + 1) if k > reach else (first + 1, first)
    return jnp.where(upward, got[a][part], got[b][part])


def pack_kernel(odd_ref, pos_h, charge_h, count_h, multi_h, leaf_h, far_h, slot_h, pair_h, *refs):
    out_refs = refs[:PEERS]
    ints_ref = refs[PEERS]
    pos, charge, count, multi_ref, leaf, far_s, slot, pair, sems = refs[PEERS + 1:]
    for c in fetch([(pos_h, pos), (charge_h, charge), (count_h, count), (multi_h, multi_ref), (leaf_h, leaf), (far_h, far_s), (slot_h, slot), (pair_h, pair)], sems):
        c.wait()
    live = iota((LEAVES, LANES), 1).astype(F32) < column(count[...])
    masked = jnp.where(live, charge[...].astype(F32), 0.0).astype(BF16)
    table = jnp.concatenate([pos[0], pos[1], pos[2], masked], axis=1)
    box = iota((LEAVES, CAP), 0)
    boxm = iota((LEAVES, CAPM), 0)
    multi = multi_ref[...]
    even = odd_ref[0] == 0
    for i, (low, high) in enumerate(routes()):
        leaf_row = jnp.where(even, leaf[high:high + 1, :], leaf[low:low + 1, :])
        far_row = jnp.where(even, far_s[high:high + 1, :], far_s[low:low + 1, :])
        pick = jnp.where(box == leaf_row, 1.0, 0.0).astype(BF16)
        rows = dot(pick, table, ((0,), (0,))).astype(BF16)
        for c in range(4):
            out_refs[i][c * CAP:(c + 1) * CAP, :] = rows[:, c * LANES:(c + 1) * LANES]
        pickm = jnp.where(boxm == far_row, 1.0, 0.0).astype(BF16)
        out_refs[i][4 * CAP:4 * CAP + CAPM, :] = dot(pickm, multi, ((0,), (0,))).astype(BF16)
    for c in range(3):
        out_refs[0][PAYLOAD + c * LEAVES:PAYLOAD + (c + 1) * LEAVES, :] = pos[c]
    ints_ref[...] = jnp.zeros_like(ints_ref)
    ints_ref[0:OPS, :] = slot[...]
    ints_ref[80:80 + COLUMNS, :] = pair[...]
    ints_ref[88:89, :] = count[...]


def pack(odd, planes, charges, count_row, multi, leaf_send, far_send, far_slots, pair_slots):
    return pl.pallas_call(
        pack_kernel,
        out_shape=[jax.ShapeDtypeStruct((PAYLOAD + 3 * LEAVES, LANES), BF16)]
        + [jax.ShapeDtypeStruct((PAYLOAD, LANES), BF16)] * (PEERS - 1) + [jax.ShapeDtypeStruct((96, LEAVES), I32)],
        in_specs=[SM] + [HBM] * 8,
        out_specs=[VM] * (PEERS + 1),
        scratch_shapes=[
            pltpu.VMEM((3, LEAVES, LANES), BF16), pltpu.VMEM((LEAVES, LANES), BF16), pltpu.VMEM((1, LEAVES), I32),
            pltpu.VMEM((LEAVES, LANES), BF16), pltpu.VMEM((PEERS, CAP), I32), pltpu.VMEM((PEERS, CAPM), I32),
            pltpu.VMEM((OPS, LEAVES), I32), pltpu.VMEM((COLUMNS, LEAVES), I32), pltpu.SemaphoreType.DMA((8,)),
        ],
        compiler_params=params(56),
        name="pack",
    )(odd, planes, charges, count_row, multi, leaf_send, far_send, far_slots, pair_slots)


def squares(x, y, z, bias):
    x, y, z = x.astype(F32), y.astype(F32), z.astype(F32)
    total = x * x + y * y + z * z + bias
    hi = total.astype(BF16)
    rest = total - hi.astype(F32)
    mid = rest.astype(BF16)
    return hi, mid, (rest - mid.astype(F32)).astype(BF16)


def spread(transposed, scale, order):
    shape = (128, 256) if transposed else (256, 128)
    big, small = iota(shape, 1 if transposed else 0), iota(shape, 0 if transposed else 1)
    feature, item = big & 15, big >> 4
    plane, item2 = small >> 4, small & 15
    value = jnp.zeros(shape, F32)
    for f, (p, v) in enumerate(order):
        value = jnp.where((feature == f) & (plane == p), v * scale if p < 3 else v, value)
    return jnp.where(item == item2, value, 0.0).astype(BF16)


def prep_kernel(own_in_ref, ints_ref, lhs_ref, order_ref, code_ref, base_ref, pair_ref, own_ref):
    own_ref[...] = own_in_ref[:PAYLOAD, :]
    count = ints_ref[88:89, :]
    pair = ints_ref[80:80 + COLUMNS, :]
    leaf_row = iota((1, LEAVES), 1).astype(F32)
    key_row = count.astype(F32) * LEAVES + leaf_row
    key_col = jnp.broadcast_to(key_row, (8, LEAVES)).T[:, 0:1]
    rank = jnp.sum(jnp.where(key_col > key_row, 1.0, 0.0), axis=0, keepdims=True)
    move = jnp.where(rank == iota((LEAVES, LEAVES), 0).astype(F32), 1.0, 0.0).astype(BF16)
    order_ref[...] = dot(jnp.broadcast_to(leaf_row, (8, LEAVES)).astype(BF16), move, ((1,), (1,))).astype(I32)
    pair_ref[:COLUMNS, :] = jnp.where(pair < 0, SLOTS, pair)
    pair_ref[COLUMNS:, :] = count
    x, y, z = [dot(move, own_in_ref[PAYLOAD + c * LEAVES:PAYLOAD + (c + 1) * LEAVES, :]).astype(BF16) for c in range(3)]
    hi, mid, lo = squares(x, y, z, 0.0)
    one = jnp.ones((16, LANES), BF16)
    zero = jnp.zeros((16, LANES), BF16)
    layout = spread(True, 1.0, [(0, 1.0), (1, 1.0), (2, 1.0), (6, 1.0), (6, 1.0), (6, 1.0), (3, 1.0), (4, 1.0), (5, 1.0)])
    for g in range(LEAVES // 16):
        at = slice(g * 16, g * 16 + 16)
        stack = jnp.concatenate([x[at], y[at], z[at], hi[at], mid[at], lo[at], one, zero], axis=0)
        feat = dot(stack, layout, ((0,), (0,)))
        lhs_ref[2 * g] = feat[:, :LANES].astype(BF16)
        lhs_ref[2 * g + 1] = feat[:, LANES:].astype(BF16)
    s = ints_ref[0:OPS, :]
    base = jnp.int32(0)
    place = s
    for k in range(PEERS):
        here = (s >= k * CAPM) & (s < (k + 1) * CAPM)
        count_k = jnp.max(jnp.where(here, s - (k * CAPM - 1), 0))
        base_ref[k] = base
        place = jnp.where(here, s + (base - k * CAPM), place)
        base = base + ((count_k + 15) & -16)
    base_ref[PEERS] = base
    row = ((place >> 9) << 8) + (place & 255)
    power = jnp.where(row >= 512, 16.0, 1.0) * jnp.where((row & 256) > 0, 4.0, 1.0) * jnp.where((row & 128) > 0, 2.0, 1.0)
    code = (1.0 + (row & 127).astype(F32) * (1.0 / 128.0)) * power
    code = jnp.where((place & 256) > 0, -code, code)
    code = jnp.where(s >= 0, code, 0.0)
    dead = jnp.zeros((1, LEAVES), F32)
    last = (CHUNKS - 1) * CHUNK
    code = jnp.concatenate([code[:last], dead, code[last:], jnp.zeros((LANES - CHUNKS * CHUNK, LEAVES), F32)], axis=0)
    code_ref[...] = code.T


def prep(own, ints):
    return pl.pallas_call(
        prep_kernel,
        out_shape=[
            jax.ShapeDtypeStruct((LEAVES // 8, LANES, LANES), BF16), jax.ShapeDtypeStruct((8, LEAVES), I32),
            jax.ShapeDtypeStruct((LEAVES, LANES), F32), jax.ShapeDtypeStruct((16,), I32),
            jax.ShapeDtypeStruct((COLUMNS + 1, LEAVES), I32), jax.ShapeDtypeStruct((PAYLOAD, LANES), BF16),
        ],
        in_specs=[VM] * 2,
        out_specs=[VM, VM, VM, SM, VM, VM],
        compiler_params=params(24),
        name="prep",
    )(own, ints)


def near_kernel(odd_ref, order, slot, lhs_ref, *refs):
    got = refs[:PEERS]
    out_ref, w_ref, q_ref = refs[PEERS:]
    one = jnp.ones((16, LANES), BF16)
    zero = jnp.zeros((16, LANES), BF16)
    layout = spread(False, -2.0, [(0, 1.0), (1, 1.0), (2, 1.0), (3, 1.0), (4, 1.0), (5, 1.0), (6, 1.0), (6, 1.0), (6, 1.0)])
    for k in range(PEERS):
        x, y, z, q = [arrived(odd_ref[0], got, k, slice(c * CAP, (c + 1) * CAP)) for c in range(4)]
        hi, mid, lo = squares(x, y, z, 0.09)
        q_ref[k * CAP:(k + 1) * CAP, :] = q.astype(F32)
        for g in range(CAP // 16):
            at = slice(g * 16, g * 16 + 16)
            stack = jnp.concatenate([x[at], y[at], z[at], hi[at], mid[at], lo[at], one, zero], axis=0)
            w_ref[k * CAP + g * 16:k * CAP + g * 16 + 16] = dot(layout, stack).astype(BF16).reshape(16, 16, LANES)
    w_ref[SLOTS] = one
    q_ref[SLOTS:SLOTS + 8, :] = jnp.zeros((8, LANES), F32)
    lane_row = iota((1, LANES), 1)
    group = 32

    def pair(g, p, rows):
        lhs = lhs_ref[group // 8 * g + p // 4][:rows, p % 4 * 32:p % 4 * 32 + 32]
        p = g * (group // 2) + p
        tiles, charge, leaf = [], [], []
        for a in range(2):
            leaf.append(order[0, 2 * p + a])
            for n in range(COLUMNS):
                s = slot[n, leaf[a]]
                t = w_ref[s]
                tiles.append(jnp.concatenate([t, zero] if a == 0 else [zero, t], axis=0))
                charge.append(q_ref[pl.ds(s, 1), :])
        acc = [None, None]
        for i in range(0, 2 * COLUMNS, 2):
            inv = lax.rsqrt(dot(lhs, jnp.concatenate(tiles[i:i + 2], axis=1)))
            for j in (i, i + 1):
                a = j // COLUMNS
                term = inv[:, (j - i) * LANES:(j - i + 1) * LANES] * charge[j]
                acc[a] = term if acc[a] is None else acc[a] + term
        for a in range(2):
            row = jnp.sum(acc[a].T, axis=0, keepdims=True)
            if rows < LANES:
                row = jnp.concatenate([row, jnp.zeros((1, LANES - rows), F32)], axis=1)
            out_ref[pl.ds(leaf[a], 1), :] = jnp.where(lane_row < slot[COLUMNS, leaf[a]], row, 0.0)

    def body(g, _):
        most = slot[COLUMNS, order[0, g * group]]
        for rows in range(STEP, LANES + 1, STEP):
            @pl.when((most > rows - STEP) & (most <= rows))
            def _():
                for p in range(group // 2):
                    pair(g, p, rows)
        return 0

    lax.fori_loop(0, LEAVES // group, body, 0)


STEP = 32


def near(odd, order, pair, lhs, got):
    return pl.pallas_call(
        near_kernel,
        out_shape=jax.ShapeDtypeStruct((LEAVES, LANES), F32),
        in_specs=[SM] * 3 + [VM] * (1 + PEERS),
        out_specs=VM,
        scratch_shapes=[
            pltpu.VMEM((SLOTS + 1, 16, LANES), BF16), pltpu.VMEM((SLOTS + 8, LANES), F32),
        ],
        compiler_params=params(24),
        name="near",
    )(odd, order, pair, lhs, *got)


def far_kernel(tile_ref, odd_ref, base_ref, code_ref, m2l_h, near_ref, *refs):
    got = refs[:PEERS]
    part_refs = refs[PEERS:PEERS + 4]
    local, table, whole, m2l, sems = refs[PEERS + 4:]
    copies = fetch([(m2l_h, m2l)], sems)
    table[...] = jnp.zeros_like(table)
    for k in range(PEERS):
        multi = arrived(odd_ref[0], got, k, slice(4 * CAP, 4 * CAP + CAPM))
        for b in range(CAPM // 16):
            at = base_ref[k] + 16 * b
            row = pl.multiple_of(((at >> 9) << 8) + (at & 255), 16)
            table[(at >> 8) & 1, pl.ds(row, 16), :] = multi[16 * b:16 * b + 16]
    local[...] = jnp.zeros_like(local)
    whole[:, :LANES] = table[0]
    whole[:, LANES:] = table[1]
    lane = iota((1, LANES), 1).astype(F32) * (1.0 / 128.0) + 1.0

    def run(depth):
        marks = [jnp.broadcast_to((lane * (2.0 ** j)).astype(BF16), (LEAVES, LANES)) for j in range(depth // LANES)]

        def body(c, _):
            code = pltpu.roll(code_ref[...], lax.rem(LANES - c * CHUNK, LANES), 1)[:, :CHUNK]
            weights = whole[:depth]
            mats = m2l[pl.ds(jnp.minimum(c * CHUNK, OPS - CHUNK), CHUNK)].reshape(CHUNK * LANES, LANES)
            rows = []
            for i in range(CHUNK):
                col = jnp.broadcast_to(code[:, i:i + 1], (LEAVES, LANES))
                wide = jnp.abs(col.astype(BF16))
                hot = jnp.concatenate([jnp.where(wide == m, jnp.ones_like(wide), jnp.zeros_like(wide)) for m in marks], axis=1)
                both = dot(hot, weights)
                rows.append(jnp.where(col < 0.0, both[:, LANES:], both[:, :LANES]).astype(BF16))
            total = local[...]
            for i in range(0, CHUNK, 8):
                total = total + dot(jnp.concatenate(rows[i:i + 8], axis=1), mats[i * LANES:(i + 8) * LANES])
            local[...] = total
            return 0

        lax.fori_loop(0, CHUNKS, body, 0)

    for c in copies:
        c.wait()
    small = base_ref[PEERS] <= 1536

    @pl.when(small)
    def _():
        run(768)

    @pl.when(jnp.logical_not(small))
    def _():
        run(1024)

    rows = LEAVES // 4
    for d in range(4):
        at = pl.multiple_of(lax.rem(tile_ref[0] + d, 4) * rows, rows)
        part_refs[d][:, :LANES] = near_ref[pl.ds(at, rows), :]
        part_refs[d][:, LANES:] = local[pl.ds(at, rows), :]


def far(tile, odd, base, code, m2l, near_part, got):
    return pl.pallas_call(
        far_kernel,
        out_shape=[jax.ShapeDtypeStruct((LEAVES // 4, 2 * LANES), F32)] * 4,
        in_specs=[SM, SM, SM, VM, HBM, VM] + [VM] * PEERS,
        out_specs=[VM] * 4,
        scratch_shapes=[
            pltpu.VMEM((LEAVES, LANES), F32), pltpu.VMEM((2, TABLE, LANES), BF16),
            pltpu.VMEM((TABLE, 2 * LANES), BF16),
            pltpu.VMEM((OPS, LANES, LANES), BF16), pltpu.SemaphoreType.DMA((1,)),
        ],
        compiler_params=params(32),
        name="far",
    )(tile, odd, base, code, m2l, near_part, *got)


def per_device(positions, charges, leaf_counts, multipoles, m2l_ops, leaf_send, pair_slots, far_send, far_slots):
    reach = (PEERS - 1) // 2
    slabs = lax.axis_size("slab")
    tiles = lax.axis_size("tile")
    planes = jnp.transpose(positions, (1, 0, 2))
    count_row = leaf_counts.reshape(1, LEAVES)
    odd = lax.rem(lax.axis_index("slab").astype(I32), 2).reshape(1)
    *payload, ints = pack(
        odd, planes, charges, count_row, multipoles, leaf_send, far_send, far_slots.T, pair_slots.T)
    got = list(payload)
    for i, (low, high) in enumerate(routes()):
        hops = high - reach
        if hops:
            pairs = [(s, (s + (hops if s % 2 == 0 else -hops)) % slabs) for s in range(slabs)]
            got[i] = lax.ppermute(payload[i], "slab", pairs)
    lhs, order, code, base, pair, got[0] = prep(payload[0], ints)
    near_part = near(odd, order, pair, lhs, got)
    tile = lax.axis_index("tile").astype(I32).reshape(1)
    parts = far(tile, odd, base, code, m2l_ops, near_part, got)
    total = parts[0]
    for step in range(1, tiles):
        total = total + lax.ppermute(parts[step], "tile", [(t, (t + step) % tiles) for t in range(tiles)])
    return total[:, :LANES], total[:, LANES:]


def solution(mesh):
    return jax.shard_map(
        per_device,
        mesh=mesh,
        in_specs=(
            P("slab", None, None),
            P("slab", None),
            P("slab"),
            P("slab", None),
            P("tile", None, None),
            P("slab", "tile"),
            P("slab", "tile"),
            P("slab", "tile"),
            P("slab", "tile"),
        ),
        out_specs=(P(("slab", "tile"), None), P(("slab", "tile"), None)),
        check_vma=False,
    )
```

```python
import jax
import jax.numpy as jnp
from jax import lax
from jax.experimental import pallas as pl
from jax.experimental.pallas import tpu as pltpu
from jax.sharding import PartitionSpec as P

F32 = jnp.float32
BF16 = jnp.bfloat16
I32 = jnp.int32
PEERS, CAP, CAPM = 9, 64, 192
LEAVES, LANES = 256, 128
COLUMNS, OPS = 7, 79
SLOTS = PEERS * CAP
PAYLOAD = 4 * CAP + CAPM
CHUNK = 40
CHUNKS = 2
TABLE = 1024
HBM = pl.BlockSpec(memory_space=pltpu.HBM)
VM = pl.BlockSpec(memory_space=pltpu.VMEM)
SM = pl.BlockSpec(memory_space=pltpu.SMEM)


def dot(a, b, dims=((1,), (0,))):
    return lax.dot_general(a, b, (dims, ((), ())), preferred_element_type=F32)


def iota(shape, dim):
    return lax.broadcasted_iota(I32, shape, dim)


def fetch(pairs, sems):
    copies = [pltpu.make_async_copy(a, b, sems.at[i]) for i, (a, b) in enumerate(pairs)]
    for c in copies:
        c.start()
    return copies


def params(mb):
    return pltpu.CompilerParams(vmem_limit_bytes=mb * 1024 * 1024)


def column(row):
    return jnp.broadcast_to(row.astype(F32), (8, LEAVES)).T[:, 0:1]


def routes():
    reach = (PEERS - 1) // 2
    pairs = [(reach, reach)]
    for step in range(reach, 0, -1):
        pairs += [(reach - step, reach + step), (reach + step, reach - step)]
    return pairs


def arrived(odd, got, k, part):
    reach = (PEERS - 1) // 2
    if k == reach:
        return got[0][part]
    step = abs(k - reach)
    first = 1 + 2 * (reach - step)
    upward = odd == step % 2
    a, b = (first, first + 1) if k > reach else (first + 1, first)
    return jnp.where(upward, got[a][part], got[b][part])


def pack_kernel(odd_ref, pos_h, charge_h, count_h, multi_h, leaf_h, far_h, slot_h, pair_h, *refs):
    out_refs = refs[:PEERS]
    ints_ref = refs[PEERS]
    pos, charge, count, multi_ref, leaf, far_s, slot, pair, sems = refs[PEERS + 1:]
    for c in fetch([(pos_h, pos), (charge_h, charge), (count_h, count), (multi_h, multi_ref), (leaf_h, leaf), (far_h, far_s), (slot_h, slot), (pair_h, pair)], sems):
        c.wait()
    live = iota((LEAVES, LANES), 1).astype(F32) < column(count[...])
    masked = jnp.where(live, charge[...].astype(F32), 0.0).astype(BF16)
    table = jnp.concatenate([pos[0], pos[1], pos[2], masked], axis=1)
    box = iota((LEAVES, CAP), 0)
    boxm = iota((LEAVES, CAPM), 0)
    multi = multi_ref[...]
    even = odd_ref[0] == 0
    for i, (low, high) in enumerate(routes()):
        leaf_row = jnp.where(even, leaf[high:high + 1, :], leaf[low:low + 1, :])
        far_row = jnp.where(even, far_s[high:high + 1, :], far_s[low:low + 1, :])
        pick = jnp.where(box == leaf_row, 1.0, 0.0).astype(BF16)
        rows = dot(pick, table, ((0,), (0,))).astype(BF16)
        for c in range(4):
            out_refs[i][c * CAP:(c + 1) * CAP, :] = rows[:, c * LANES:(c + 1) * LANES]
        pickm = jnp.where(boxm == far_row, 1.0, 0.0).astype(BF16)
        out_refs[i][4 * CAP:4 * CAP + CAPM, :] = dot(pickm, multi, ((0,), (0,))).astype(BF16)
    for c in range(3):
        out_refs[0][PAYLOAD + c * LEAVES:PAYLOAD + (c + 1) * LEAVES, :] = pos[c]
    ints_ref[...] = jnp.zeros_like(ints_ref)
    ints_ref[0:OPS, :] = slot[...]
    ints_ref[80:80 + COLUMNS, :] = pair[...]
    ints_ref[88:89, :] = count[...]


def pack(odd, planes, charges, count_row, multi, leaf_send, far_send, far_slots, pair_slots):
    return pl.pallas_call(
        pack_kernel,
        out_shape=[jax.ShapeDtypeStruct((PAYLOAD + 3 * LEAVES, LANES), BF16)]
        + [jax.ShapeDtypeStruct((PAYLOAD, LANES), BF16)] * (PEERS - 1) + [jax.ShapeDtypeStruct((96, LEAVES), I32)],
        in_specs=[SM] + [HBM] * 8,
        out_specs=[VM] * (PEERS + 1),
        scratch_shapes=[
            pltpu.VMEM((3, LEAVES, LANES), BF16), pltpu.VMEM((LEAVES, LANES), BF16), pltpu.VMEM((1, LEAVES), I32),
            pltpu.VMEM((LEAVES, LANES), BF16), pltpu.VMEM((PEERS, CAP), I32), pltpu.VMEM((PEERS, CAPM), I32),
            pltpu.VMEM((OPS, LEAVES), I32), pltpu.VMEM((COLUMNS, LEAVES), I32), pltpu.SemaphoreType.DMA((8,)),
        ],
        compiler_params=params(56),
        name="pack",
    )(odd, planes, charges, count_row, multi, leaf_send, far_send, far_slots, pair_slots)


def squares(x, y, z, bias):
    x, y, z = x.astype(F32), y.astype(F32), z.astype(F32)
    total = x * x + y * y + z * z + bias
    hi = total.astype(BF16)
    rest = total - hi.astype(F32)
    mid = rest.astype(BF16)
    return hi, mid, (rest - mid.astype(F32)).astype(BF16)


def spread(transposed, scale, order):
    shape = (128, 256) if transposed else (256, 128)
    big, small = iota(shape, 1 if transposed else 0), iota(shape, 0 if transposed else 1)
    feature, item = big & 15, big >> 4
    plane, item2 = small >> 4, small & 15
    value = jnp.zeros(shape, F32)
    for f, (p, v) in enumerate(order):
        value = jnp.where((feature == f) & (plane == p), v * scale if p < 3 else v, value)
    return jnp.where(item == item2, value, 0.0).astype(BF16)


def prep_kernel(own_in_ref, ints_ref, lhs_ref, order_ref, code_ref, base_ref, pair_ref, own_ref):
    own_ref[...] = own_in_ref[:PAYLOAD, :]
    count = ints_ref[88:89, :]
    pair = ints_ref[80:80 + COLUMNS, :]
    leaf_row = iota((1, LEAVES), 1).astype(F32)
    key_row = count.astype(F32) * LEAVES + leaf_row
    key_col = jnp.broadcast_to(key_row, (8, LEAVES)).T[:, 0:1]
    rank = jnp.sum(jnp.where(key_col > key_row, 1.0, 0.0), axis=0, keepdims=True)
    move = jnp.where(rank == iota((LEAVES, LEAVES), 0).astype(F32), 1.0, 0.0).astype(BF16)
    order_ref[...] = dot(jnp.broadcast_to(leaf_row, (8, LEAVES)).astype(BF16), move, ((1,), (1,))).astype(I32)
    pair_ref[:COLUMNS, :] = jnp.where(pair < 0, SLOTS, pair)
    pair_ref[COLUMNS:, :] = count
    x, y, z = [dot(move, own_in_ref[PAYLOAD + c * LEAVES:PAYLOAD + (c + 1) * LEAVES, :]).astype(BF16) for c in range(3)]
    hi, mid, lo = squares(x, y, z, 0.0)
    one = jnp.ones((16, LANES), BF16)
    zero = jnp.zeros((16, LANES), BF16)
    layout = spread(True, 1.0, [(0, 1.0), (1, 1.0), (2, 1.0), (6, 1.0), (6, 1.0), (6, 1.0), (3, 1.0), (4, 1.0), (5, 1.0)])
    for g in range(LEAVES // 16):
        at = slice(g * 16, g * 16 + 16)
        stack = jnp.concatenate([x[at], y[at], z[at], hi[at], mid[at], lo[at], one, zero], axis=0)
        feat = dot(stack, layout, ((0,), (0,)))
        lhs_ref[2 * g] = feat[:, :LANES].astype(BF16)
        lhs_ref[2 * g + 1] = feat[:, LANES:].astype(BF16)
    s = ints_ref[0:OPS, :]
    base = jnp.int32(0)
    place = s
    for k in range(PEERS):
        here = (s >= k * CAPM) & (s < (k + 1) * CAPM)
        count_k = jnp.max(jnp.where(here, s - (k * CAPM - 1), 0))
        base_ref[k] = base
        place = jnp.where(here, s + (base - k * CAPM), place)
        base = base + ((count_k + 15) & -16)
    base_ref[PEERS] = base
    row = ((place >> 9) << 8) + (place & 255)
    power = jnp.where(row >= 512, 16.0, 1.0) * jnp.where((row & 256) > 0, 4.0, 1.0) * jnp.where((row & 128) > 0, 2.0, 1.0)
    code = (1.0 + (row & 127).astype(F32) * (1.0 / 128.0)) * power
    code = jnp.where((place & 256) > 0, -code, code)
    code = jnp.where(s >= 0, code, 0.0)
    dead = jnp.zeros((1, LEAVES), F32)
    last = (CHUNKS - 1) * CHUNK
    code = jnp.concatenate([code[:last], dead, code[last:], jnp.zeros((LANES - CHUNKS * CHUNK, LEAVES), F32)], axis=0)
    code_ref[...] = code.T


def prep(own, ints):
    return pl.pallas_call(
        prep_kernel,
        out_shape=[
            jax.ShapeDtypeStruct((LEAVES // 8, LANES, LANES), BF16), jax.ShapeDtypeStruct((8, LEAVES), I32),
            jax.ShapeDtypeStruct((LEAVES, LANES), F32), jax.ShapeDtypeStruct((16,), I32),
            jax.ShapeDtypeStruct((COLUMNS + 1, LEAVES), I32), jax.ShapeDtypeStruct((PAYLOAD, LANES), BF16),
        ],
        in_specs=[VM] * 2,
        out_specs=[VM, VM, VM, SM, VM, VM],
        compiler_params=params(24),
        name="prep",
    )(own, ints)


def near_kernel(odd_ref, order, slot, lhs_ref, *refs):
    got = refs[:PEERS]
    out_ref, w_ref, q_ref = refs[PEERS:]
    one = jnp.ones((16, LANES), BF16)
    zero = jnp.zeros((16, LANES), BF16)
    layout = spread(False, -2.0, [(0, 1.0), (1, 1.0), (2, 1.0), (3, 1.0), (4, 1.0), (5, 1.0), (6, 1.0), (6, 1.0), (6, 1.0)])
    for k in range(PEERS):
        x, y, z, q = [arrived(odd_ref[0], got, k, slice(c * CAP, (c + 1) * CAP)) for c in range(4)]
        hi, mid, lo = squares(x, y, z, 0.09)
        q_ref[k * CAP:(k + 1) * CAP, :] = q.astype(F32)
        for g in range(CAP // 16):
            at = slice(g * 16, g * 16 + 16)
            stack = jnp.concatenate([x[at], y[at], z[at], hi[at], mid[at], lo[at], one, zero], axis=0)
            w_ref[k * CAP + g * 16:k * CAP + g * 16 + 16] = dot(layout, stack).astype(BF16).reshape(16, 16, LANES)
    w_ref[SLOTS] = one
    q_ref[SLOTS:SLOTS + 8, :] = jnp.zeros((8, LANES), F32)
    lane_row = iota((1, LANES), 1)
    group = 32

    def pair(g, p, rows):
        lhs = lhs_ref[group // 8 * g + p // 4][:rows, p % 4 * 32:p % 4 * 32 + 32]
        p = g * (group // 2) + p
        tiles, charge, leaf = [], [], []
        for a in range(2):
            leaf.append(order[0, 2 * p + a])
            for n in range(COLUMNS):
                s = slot[n, leaf[a]]
                t = w_ref[s]
                tiles.append(jnp.concatenate([t, zero] if a == 0 else [zero, t], axis=0))
                charge.append(q_ref[pl.ds(s, 1), :])
        acc = [None, None]
        for i in range(0, 2 * COLUMNS, 2):
            inv = lax.rsqrt(dot(lhs, jnp.concatenate(tiles[i:i + 2], axis=1)))
            for j in (i, i + 1):
                a = j // COLUMNS
                term = inv[:, (j - i) * LANES:(j - i + 1) * LANES] * charge[j]
                acc[a] = term if acc[a] is None else acc[a] + term
        for a in range(2):
            row = jnp.sum(acc[a].T, axis=0, keepdims=True)
            if rows < LANES:
                row = jnp.concatenate([row, jnp.zeros((1, LANES - rows), F32)], axis=1)
            out_ref[pl.ds(leaf[a], 1), :] = jnp.where(lane_row < slot[COLUMNS, leaf[a]], row, 0.0)

    def body(g, _):
        most = slot[COLUMNS, order[0, g * group]]
        for rows in range(STEP, LANES + 1, STEP):
            @pl.when((most > rows - STEP) & (most <= rows))
            def _():
                for p in range(group // 2):
                    pair(g, p, rows)
        return 0

    lax.fori_loop(0, LEAVES // group, body, 0)


STEP = 32


def near(odd, order, pair, lhs, got):
    return pl.pallas_call(
        near_kernel,
        out_shape=jax.ShapeDtypeStruct((LEAVES, LANES), F32),
        in_specs=[SM] * 3 + [VM] * (1 + PEERS),
        out_specs=VM,
        scratch_shapes=[
            pltpu.VMEM((SLOTS + 1, 16, LANES), BF16), pltpu.VMEM((SLOTS + 8, LANES), F32),
        ],
        compiler_params=params(24),
        name="near",
    )(odd, order, pair, lhs, *got)


def far_kernel(tile_ref, odd_ref, base_ref, code_ref, m2l_h, near_ref, *refs):
    got = refs[:PEERS]
    part_refs = refs[PEERS:PEERS + 4]
    local, table, whole, m2l, sems = refs[PEERS + 4:]
    copies = fetch([(m2l_h, m2l)], sems)
    table[...] = jnp.zeros_like(table)
    for k in range(PEERS):
        multi = arrived(odd_ref[0], got, k, slice(4 * CAP, 4 * CAP + CAPM))
        for b in range(CAPM // 16):
            at = base_ref[k] + 16 * b
            row = pl.multiple_of(((at >> 9) << 8) + (at & 255), 16)
            table[(at >> 8) & 1, pl.ds(row, 16), :] = multi[16 * b:16 * b + 16]
    local[...] = jnp.zeros_like(local)
    whole[:, :LANES] = table[0]
    whole[:, LANES:] = table[1]
    lane = iota((1, LANES), 1).astype(F32) * (1.0 / 128.0) + 1.0

    def run(depth):
        marks = [jnp.broadcast_to((lane * (2.0 ** j)).astype(BF16), (LEAVES, LANES)) for j in range(depth // LANES)]

        def body(c, _):
            code = pltpu.roll(code_ref[...], lax.rem(LANES - c * CHUNK, LANES), 1)[:, :CHUNK]
            weights = whole[:depth]
            mats = m2l[pl.ds(jnp.minimum(c * CHUNK, OPS - CHUNK), CHUNK)].reshape(CHUNK * LANES, LANES)
            rows = []
            for i in range(CHUNK):
                col = jnp.broadcast_to(code[:, i:i + 1], (LEAVES, LANES))
                wide = jnp.abs(col.astype(BF16))
                hot = jnp.concatenate([jnp.where(wide == m, jnp.ones_like(wide), jnp.zeros_like(wide)) for m in marks], axis=1)
                both = dot(hot, weights)
                rows.append(jnp.where(col < 0.0, both[:, LANES:], both[:, :LANES]).astype(BF16))
            total = local[...]
            for i in range(0, CHUNK, 8):
                total = total + dot(jnp.concatenate(rows[i:i + 8], axis=1), mats[i * LANES:(i + 8) * LANES])
            local[...] = total
            return 0

        lax.fori_loop(0, CHUNKS, body, 0)

    for c in copies:
        c.wait()
    small = base_ref[PEERS] <= 1536

    @pl.when(small)
    def _():
        run(768)

    @pl.when(jnp.logical_not(small))
    def _():
        run(1024)

    rows = LEAVES // 4
    for d in range(4):
        at = pl.multiple_of(lax.rem(tile_ref[0] + jnp.where(odd_ref[0] == 0, d, 4 - d), 4) * rows, rows)
        part_refs[d][:, :LANES] = near_ref[pl.ds(at, rows), :]
        part_refs[d][:, LANES:] = local[pl.ds(at, rows), :]


def far(tile, odd, base, code, m2l, near_part, got):
    return pl.pallas_call(
        far_kernel,
        out_shape=[jax.ShapeDtypeStruct((LEAVES // 4, 2 * LANES), F32)] * 4,
        in_specs=[SM, SM, SM, VM, HBM, VM] + [VM] * PEERS,
        out_specs=[VM] * 4,
        scratch_shapes=[
            pltpu.VMEM((LEAVES, LANES), F32), pltpu.VMEM((2, TABLE, LANES), BF16),
            pltpu.VMEM((TABLE, 2 * LANES), BF16),
            pltpu.VMEM((OPS, LANES, LANES), BF16), pltpu.SemaphoreType.DMA((1,)),
        ],
        compiler_params=params(32),
        name="far",
    )(tile, odd, base, code, m2l, near_part, *got)


def per_device(positions, charges, leaf_counts, multipoles, m2l_ops, leaf_send, pair_slots, far_send, far_slots):
    reach = (PEERS - 1) // 2
    slabs = lax.axis_size("slab")
    tiles = lax.axis_size("tile")
    planes = jnp.transpose(positions, (1, 0, 2))
    count_row = leaf_counts.reshape(1, LEAVES)
    odd = lax.rem(lax.axis_index("slab").astype(I32), 2).reshape(1)
    *payload, ints = pack(
        odd, planes, charges, count_row, multipoles, leaf_send, far_send, far_slots.T, pair_slots.T)
    got = list(payload)
    for i, (low, high) in enumerate(routes()):
        hops = high - reach
        if hops:
            pairs = [(s, (s + (hops if s % 2 == 0 else -hops)) % slabs) for s in range(slabs)]
            got[i] = lax.ppermute(payload[i], "slab", pairs)
    lhs, order, code, base, pair, got[0] = prep(payload[0], ints)
    near_part = near(odd, order, pair, lhs, got)
    tile = lax.axis_index("tile").astype(I32).reshape(1)
    parts = far(tile, odd, base, code, m2l_ops, near_part, got)
    total = parts[0]
    for step in range(1, tiles):
        pairs = [
            (r * tiles + t, r * tiles + (t + (step if r % 2 == 0 else -step)) % tiles)
            for r in range(slabs) for t in range(tiles)
        ]
        total = total + lax.ppermute(parts[step], ("slab", "tile"), pairs)
    return total[:, :LANES], total[:, LANES:]


def solution(mesh):
    return jax.shard_map(
        per_device,
        mesh=mesh,
        in_specs=(
            P("slab", None, None),
            P("slab", None),
            P("slab"),
            P("slab", None),
            P("tile", None, None),
            P("slab", "tile"),
            P("slab", "tile"),
            P("slab", "tile"),
            P("slab", "tile"),
        ),
        out_specs=(P(("slab", "tile"), None), P(("slab", "tile"), None)),
        check_vma=False,
    )
```

```python
import jax
import jax.numpy as jnp
from jax import lax
from jax.experimental import pallas as pl
from jax.experimental.pallas import tpu as pltpu
from jax.sharding import PartitionSpec as P

F32 = jnp.float32
BF16 = jnp.bfloat16
I32 = jnp.int32
PEERS, CAP, CAPM = 9, 64, 192
LEAVES, LANES = 256, 128
COLUMNS, OPS = 7, 79
SLOTS = PEERS * CAP
PAYLOAD = 4 * CAP + CAPM
CHUNK = 40
CHUNKS = 2
TABLE = 1024
HBM = pl.BlockSpec(memory_space=pltpu.HBM)
VM = pl.BlockSpec(memory_space=pltpu.VMEM)
SM = pl.BlockSpec(memory_space=pltpu.SMEM)


def dot(a, b, dims=((1,), (0,))):
    return lax.dot_general(a, b, (dims, ((), ())), preferred_element_type=F32)


def iota(shape, dim):
    return lax.broadcasted_iota(I32, shape, dim)


def fetch(pairs, sems):
    copies = [pltpu.make_async_copy(a, b, sems.at[i]) for i, (a, b) in enumerate(pairs)]
    for c in copies:
        c.start()
    return copies


def params(mb):
    return pltpu.CompilerParams(vmem_limit_bytes=mb * 1024 * 1024)


def column(row):
    return jnp.broadcast_to(row.astype(F32), (8, LEAVES)).T[:, 0:1]


def routes():
    reach = (PEERS - 1) // 2
    pairs = [(reach, reach)]
    for step in range(reach, 0, -1):
        pair = [(reach - step, reach + step), (reach + step, reach - step)]
        pairs += pair[::-1] if step == 1 else pair
    return pairs


def arrived(odd, got, k, part):
    reach = (PEERS - 1) // 2
    if k == reach:
        return got[0][part]
    step = abs(k - reach)
    first = 1 + 2 * (reach - step)
    upward = odd == step % 2
    a, b = (first, first + 1) if (k > reach) != (step == 1) else (first + 1, first)
    return jnp.where(upward, got[a][part], got[b][part])


def pack_kernel(odd_ref, pos_h, charge_h, count_h, multi_h, leaf_h, far_h, slot_h, pair_h, *refs):
    out_refs = refs[:PEERS]
    ints_ref = refs[PEERS]
    pos, charge, count, multi_ref, leaf, far_s, slot, pair, sems = refs[PEERS + 1:]
    for c in fetch([(pos_h, pos), (charge_h, charge), (count_h, count), (multi_h, multi_ref), (leaf_h, leaf), (far_h, far_s), (slot_h, slot), (pair_h, pair)], sems):
        c.wait()
    live = iota((LEAVES, LANES), 1).astype(F32) < column(count[...])
    masked = jnp.where(live, charge[...].astype(F32), 0.0).astype(BF16)
    table = jnp.concatenate([pos[0], pos[1], pos[2], masked], axis=1)
    box = iota((LEAVES, CAP), 0)
    boxm = iota((LEAVES, CAPM), 0)
    multi = multi_ref[...]
    even = odd_ref[0] == 0
    for i, (low, high) in enumerate(routes()):
        leaf_row = jnp.where(even, leaf[high:high + 1, :], leaf[low:low + 1, :])
        far_row = jnp.where(even, far_s[high:high + 1, :], far_s[low:low + 1, :])
        pick = jnp.where(box == leaf_row, 1.0, 0.0).astype(BF16)
        rows = dot(pick, table, ((0,), (0,))).astype(BF16)
        for c in range(4):
            out_refs[i][c * CAP:(c + 1) * CAP, :] = rows[:, c * LANES:(c + 1) * LANES]
        pickm = jnp.where(boxm == far_row, 1.0, 0.0).astype(BF16)
        out_refs[i][4 * CAP:4 * CAP + CAPM, :] = dot(pickm, multi, ((0,), (0,))).astype(BF16)
    for c in range(3):
        out_refs[0][PAYLOAD + c * LEAVES:PAYLOAD + (c + 1) * LEAVES, :] = pos[c]
    ints_ref[...] = jnp.zeros_like(ints_ref)
    ints_ref[0:OPS, :] = slot[...]
    ints_ref[80:80 + COLUMNS, :] = pair[...]
    ints_ref[88:89, :] = count[...]


def pack(odd, planes, charges, count_row, multi, leaf_send, far_send, far_slots, pair_slots):
    return pl.pallas_call(
        pack_kernel,
        out_shape=[jax.ShapeDtypeStruct((PAYLOAD + 3 * LEAVES, LANES), BF16)]
        + [jax.ShapeDtypeStruct((PAYLOAD, LANES), BF16)] * (PEERS - 1) + [jax.ShapeDtypeStruct((96, LEAVES), I32)],
        in_specs=[SM] + [HBM] * 8,
        out_specs=[VM] * (PEERS + 1),
        scratch_shapes=[
            pltpu.VMEM((3, LEAVES, LANES), BF16), pltpu.VMEM((LEAVES, LANES), BF16), pltpu.VMEM((1, LEAVES), I32),
            pltpu.VMEM((LEAVES, LANES), BF16), pltpu.VMEM((PEERS, CAP), I32), pltpu.VMEM((PEERS, CAPM), I32),
            pltpu.VMEM((OPS, LEAVES), I32), pltpu.VMEM((COLUMNS, LEAVES), I32), pltpu.SemaphoreType.DMA((8,)),
        ],
        compiler_params=params(56),
        name="pack",
    )(odd, planes, charges, count_row, multi, leaf_send, far_send, far_slots, pair_slots)


def squares(x, y, z, bias):
    x, y, z = x.astype(F32), y.astype(F32), z.astype(F32)
    total = x * x + y * y + z * z + bias
    hi = total.astype(BF16)
    rest = total - hi.astype(F32)
    mid = rest.astype(BF16)
    return hi, mid, (rest - mid.astype(F32)).astype(BF16)


def spread(transposed, scale, order):
    shape = (128, 256) if transposed else (256, 128)
    big, small = iota(shape, 1 if transposed else 0), iota(shape, 0 if transposed else 1)
    feature, item = big & 15, big >> 4
    plane, item2 = small >> 4, small & 15
    value = jnp.zeros(shape, F32)
    for f, (p, v) in enumerate(order):
        value = jnp.where((feature == f) & (plane == p), v * scale if p < 3 else v, value)
    return jnp.where(item == item2, value, 0.0).astype(BF16)


def prep_kernel(own_in_ref, ints_ref, lhs_ref, order_ref, code_ref, base_ref, pair_ref, own_ref):
    own_ref[...] = own_in_ref[:PAYLOAD, :]
    count = ints_ref[88:89, :]
    pair = ints_ref[80:80 + COLUMNS, :]
    leaf_row = iota((1, LEAVES), 1).astype(F32)
    key_row = count.astype(F32) * LEAVES + leaf_row
    key_col = jnp.broadcast_to(key_row, (8, LEAVES)).T[:, 0:1]
    rank = jnp.sum(jnp.where(key_col > key_row, 1.0, 0.0), axis=0, keepdims=True)
    move = jnp.where(rank == iota((LEAVES, LEAVES), 0).astype(F32), 1.0, 0.0).astype(BF16)
    order_ref[...] = dot(jnp.broadcast_to(leaf_row, (8, LEAVES)).astype(BF16), move, ((1,), (1,))).astype(I32)
    pair_ref[:COLUMNS, :] = jnp.where(pair < 0, SLOTS, pair)
    pair_ref[COLUMNS:, :] = count
    x, y, z = [dot(move, own_in_ref[PAYLOAD + c * LEAVES:PAYLOAD + (c + 1) * LEAVES, :]).astype(BF16) for c in range(3)]
    hi, mid, lo = squares(x, y, z, 0.0)
    one = jnp.ones((16, LANES), BF16)
    zero = jnp.zeros((16, LANES), BF16)
    layout = spread(True, 1.0, [(0, 1.0), (1, 1.0), (2, 1.0), (6, 1.0), (6, 1.0), (6, 1.0), (3, 1.0), (4, 1.0), (5, 1.0)])
    for g in range(LEAVES // 16):
        at = slice(g * 16, g * 16 + 16)
        stack = jnp.concatenate([x[at], y[at], z[at], hi[at], mid[at], lo[at], one, zero], axis=0)
        feat = dot(stack, layout, ((0,), (0,)))
        lhs_ref[2 * g] = feat[:, :LANES].astype(BF16)
        lhs_ref[2 * g + 1] = feat[:, LANES:].astype(BF16)
    s = ints_ref[0:OPS, :]
    base = jnp.int32(0)
    place = s
    for k in range(PEERS):
        here = (s >= k * CAPM) & (s < (k + 1) * CAPM)
        count_k = jnp.max(jnp.where(here, s - (k * CAPM - 1), 0))
        base_ref[k] = base
        place = jnp.where(here, s + (base - k * CAPM), place)
        base = base + ((count_k + 15) & -16)
    base_ref[PEERS] = base
    row = ((place >> 9) << 8) + (place & 255)
    power = jnp.where(row >= 512, 16.0, 1.0) * jnp.where((row & 256) > 0, 4.0, 1.0) * jnp.where((row & 128) > 0, 2.0, 1.0)
    code = (1.0 + (row & 127).astype(F32) * (1.0 / 128.0)) * power
    code = jnp.where((place & 256) > 0, -code, code)
    code = jnp.where(s >= 0, code, 0.0)
    dead = jnp.zeros((1, LEAVES), F32)
    last = (CHUNKS - 1) * CHUNK
    code = jnp.concatenate([code[:last], dead, code[last:], jnp.zeros((LANES - CHUNKS * CHUNK, LEAVES), F32)], axis=0)
    code_ref[...] = code.T


def prep(own, ints):
    return pl.pallas_call(
        prep_kernel,
        out_shape=[
            jax.ShapeDtypeStruct((LEAVES // 8, LANES, LANES), BF16), jax.ShapeDtypeStruct((8, LEAVES), I32),
            jax.ShapeDtypeStruct((LEAVES, LANES), F32), jax.ShapeDtypeStruct((16,), I32),
            jax.ShapeDtypeStruct((COLUMNS + 1, LEAVES), I32), jax.ShapeDtypeStruct((PAYLOAD, LANES), BF16),
        ],
        in_specs=[VM] * 2,
        out_specs=[VM, VM, VM, SM, VM, VM],
        compiler_params=params(24),
        name="prep",
    )(own, ints)


def near_kernel(odd_ref, order, slot, lhs_ref, *refs):
    got = refs[:PEERS]
    out_ref, w_ref, q_ref = refs[PEERS:]
    one = jnp.ones((16, LANES), BF16)
    zero = jnp.zeros((16, LANES), BF16)
    layout = spread(False, -2.0, [(0, 1.0), (1, 1.0), (2, 1.0), (3, 1.0), (4, 1.0), (5, 1.0), (6, 1.0), (6, 1.0), (6, 1.0)])
    for k in range(PEERS):
        x, y, z, q = [arrived(odd_ref[0], got, k, slice(c * CAP, (c + 1) * CAP)) for c in range(4)]
        hi, mid, lo = squares(x, y, z, 0.09)
        q_ref[k * CAP:(k + 1) * CAP, :] = q.astype(F32)
        for g in range(CAP // 16):
            at = slice(g * 16, g * 16 + 16)
            stack = jnp.concatenate([x[at], y[at], z[at], hi[at], mid[at], lo[at], one, zero], axis=0)
            w_ref[k * CAP + g * 16:k * CAP + g * 16 + 16] = dot(layout, stack).astype(BF16).reshape(16, 16, LANES)
    w_ref[SLOTS] = one
    q_ref[SLOTS:SLOTS + 8, :] = jnp.zeros((8, LANES), F32)
    lane_row = iota((1, LANES), 1)
    group = 32

    def pair(g, p, rows):
        lhs = lhs_ref[group // 8 * g + p // 4][:rows, p % 4 * 32:p % 4 * 32 + 32]
        p = g * (group // 2) + p
        tiles, charge, leaf = [], [], []
        for a in range(2):
            leaf.append(order[0, 2 * p + a])
            for n in range(COLUMNS):
                s = slot[n, leaf[a]]
                t = w_ref[s]
                tiles.append(jnp.concatenate([t, zero] if a == 0 else [zero, t], axis=0))
                charge.append(q_ref[pl.ds(s, 1), :])
        acc = [None, None]
        for i in range(0, 2 * COLUMNS, 2):
            inv = lax.rsqrt(dot(lhs, jnp.concatenate(tiles[i:i + 2], axis=1)))
            for j in (i, i + 1):
                a = j // COLUMNS
                term = inv[:, (j - i) * LANES:(j - i + 1) * LANES] * charge[j]
                acc[a] = term if acc[a] is None else acc[a] + term
        for a in range(2):
            row = jnp.sum(acc[a].T, axis=0, keepdims=True)
            if rows < LANES:
                row = jnp.concatenate([row, jnp.zeros((1, LANES - rows), F32)], axis=1)
            out_ref[pl.ds(leaf[a], 1), :] = jnp.where(lane_row < slot[COLUMNS, leaf[a]], row, 0.0)

    def body(g, _):
        most = slot[COLUMNS, order[0, g * group]]
        for rows in range(STEP, LANES + 1, STEP):
            @pl.when((most > rows - STEP) & (most <= rows))
            def _():
                for p in range(group // 2):
                    pair(g, p, rows)
        return 0

    lax.fori_loop(0, LEAVES // group, body, 0)


STEP = 32


def near(odd, order, pair, lhs, got):
    return pl.pallas_call(
        near_kernel,
        out_shape=jax.ShapeDtypeStruct((LEAVES, LANES), F32),
        in_specs=[SM] * 3 + [VM] * (1 + PEERS),
        out_specs=VM,
        scratch_shapes=[
            pltpu.VMEM((SLOTS + 1, 16, LANES), BF16), pltpu.VMEM((SLOTS + 8, LANES), F32),
        ],
        compiler_params=params(24),
        name="near",
    )(odd, order, pair, lhs, *got)


def far_kernel(tile_ref, odd_ref, base_ref, code_ref, m2l_h, near_ref, *refs):
    got = refs[:PEERS]
    part_refs = refs[PEERS:PEERS + 4]
    local, table, whole, m2l, sems = refs[PEERS + 4:]
    copies = fetch([(m2l_h, m2l)], sems)
    table[...] = jnp.zeros_like(table)
    for k in range(PEERS):
        multi = arrived(odd_ref[0], got, k, slice(4 * CAP, 4 * CAP + CAPM))
        for b in range(CAPM // 16):
            at = base_ref[k] + 16 * b
            row = pl.multiple_of(((at >> 9) << 8) + (at & 255), 16)
            table[(at >> 8) & 1, pl.ds(row, 16), :] = multi[16 * b:16 * b + 16]
    local[...] = jnp.zeros_like(local)
    whole[:, :LANES] = table[0]
    whole[:, LANES:] = table[1]
    lane = iota((1, LANES), 1).astype(F32) * (1.0 / 128.0) + 1.0

    def run(depth):
        marks = [jnp.broadcast_to((lane * (2.0 ** j)).astype(BF16), (LEAVES, LANES)) for j in range(depth // LANES)]

        def body(c, _):
            code = pltpu.roll(code_ref[...], lax.rem(LANES - c * CHUNK, LANES), 1)[:, :CHUNK]
            weights = whole[:depth]
            mats = m2l[pl.ds(jnp.minimum(c * CHUNK, OPS - CHUNK), CHUNK)].reshape(CHUNK * LANES, LANES)
            rows = []
            for i in range(CHUNK):
                col = jnp.broadcast_to(code[:, i:i + 1], (LEAVES, LANES))
                wide = jnp.abs(col.astype(BF16))
                hot = jnp.concatenate([jnp.where(wide == m, jnp.ones_like(wide), jnp.zeros_like(wide)) for m in marks], axis=1)
                both = dot(hot, weights)
                rows.append(jnp.where(col < 0.0, both[:, LANES:], both[:, :LANES]).astype(BF16))
            total = local[...]
            for i in range(0, CHUNK, 8):
                total = total + dot(jnp.concatenate(rows[i:i + 8], axis=1), mats[i * LANES:(i + 8) * LANES])
            local[...] = total
            return 0

        lax.fori_loop(0, CHUNKS, body, 0)

    for c in copies:
        c.wait()
    small = base_ref[PEERS] <= 1536

    @pl.when(small)
    def _():
        run(768)

    @pl.when(jnp.logical_not(small))
    def _():
        run(1024)

    rows = LEAVES // 4
    for d in range(4):
        at = pl.multiple_of(lax.rem(tile_ref[0] + jnp.where(odd_ref[0] == 0, d, 4 - d), 4) * rows, rows)
        part_refs[d][:, :LANES] = near_ref[pl.ds(at, rows), :]
        part_refs[d][:, LANES:] = local[pl.ds(at, rows), :]


def far(tile, odd, base, code, m2l, near_part, got):
    return pl.pallas_call(
        far_kernel,
        out_shape=[jax.ShapeDtypeStruct((LEAVES // 4, 2 * LANES), F32)] * 4,
        in_specs=[SM, SM, SM, VM, HBM, VM] + [VM] * PEERS,
        out_specs=[VM] * 4,
        scratch_shapes=[
            pltpu.VMEM((LEAVES, LANES), F32), pltpu.VMEM((2, TABLE, LANES), BF16),
            pltpu.VMEM((TABLE, 2 * LANES), BF16),
            pltpu.VMEM((OPS, LANES, LANES), BF16), pltpu.SemaphoreType.DMA((1,)),
        ],
        compiler_params=params(32),
        name="far",
    )(tile, odd, base, code, m2l, near_part, *got)


def per_device(positions, charges, leaf_counts, multipoles, m2l_ops, leaf_send, pair_slots, far_send, far_slots):
    reach = (PEERS - 1) // 2
    slabs = lax.axis_size("slab")
    tiles = lax.axis_size("tile")
    planes = jnp.transpose(positions, (1, 0, 2))
    count_row = leaf_counts.reshape(1, LEAVES)
    odd = lax.rem(lax.axis_index("slab").astype(I32), 2).reshape(1)
    *payload, ints = pack(
        odd, planes, charges, count_row, multipoles, leaf_send, far_send, far_slots.T, pair_slots.T)
    got = list(payload)
    for i, (low, high) in enumerate(routes()):
        hops = high - reach
        if hops:
            pairs = [(s, (s + (hops if s % 2 == 0 else -hops)) % slabs) for s in range(slabs)]
            got[i] = lax.ppermute(payload[i], "slab", pairs)
    lhs, order, code, base, pair, got[0] = prep(payload[0], ints)
    near_part = near(odd, order, pair, lhs, got)
    tile = lax.axis_index("tile").astype(I32).reshape(1)
    parts = far(tile, odd, base, code, m2l_ops, near_part, got)
    total = parts[0]
    for step in range(1, tiles):
        pairs = [
            (r * tiles + t, r * tiles + (t + (step if r % 2 == 0 else -step)) % tiles)
            for r in range(slabs) for t in range(tiles)
        ]
        total = total + lax.ppermute(parts[step], ("slab", "tile"), pairs)
    return total[:, :LANES], total[:, LANES:]


def solution(mesh):
    return jax.shard_map(
        per_device,
        mesh=mesh,
        in_specs=(
            P("slab", None, None),
            P("slab", None),
            P("slab"),
            P("slab", None),
            P("tile", None, None),
            P("slab", "tile"),
            P("slab", "tile"),
            P("slab", "tile"),
            P("slab", "tile"),
        ),
        out_specs=(P(("slab", "tile"), None), P(("slab", "tile"), None)),
        check_vma=False,
    )
```
